32 devices in a mesh: gx: 4 (over y, core), gy: 4 (over z), gz: 2 (over x).
Axes of the slice: x: 2, y: 2, z: 4, core: 2. Of those that a mesh axis runs over, the one named last changes fastest.
Arguments:
- scalars: float32 [4, 4, 2, 128, 128], P('gx', 'gy', 'gz'), may hold values from -6 to 6
- vectors: float32 [4, 4, 2, 3, 128, 128], P('gx', 'gy', 'gz'), may hold values from -6 to 6
- positions: float32 [4, 4, 2, 3, 128], P('gx', 'gy', 'gz'), may hold values from 0 to 6
- species: int32 [4, 4, 2, 128], P('gx', 'gy', 'gz'), may hold values from 0 to 7
- atom_count: int32 [4, 4, 2], P('gx', 'gy', 'gz'), may hold values from 64 to 128, as said below
- energy_weight: float32 [4, 4, 2, 128], P('gx', 'gy', 'gz'), may hold values from -5 to 5
- local_pairs: int32 [4, 4, 2, 2, 1024], P('gx', 'gy', 'gz'), may hold values from 0 to 127, as said below
- face_pairs: int32 [4, 4, 2, 3, 2, 256], P('gx', 'gy', 'gz'), may hold values from 0 to 127, as said below
- tile_counts: int32 [4, 4, 2, 4], P('gx', 'gy', 'gz'), may hold values from 85 to 1024, as said below
- w_center: float32 [128, 128], replicated, may hold values from -0.5 to 0.5
- w_partner: float32 [128, 128], replicated, may hold values from -0.5 to 0.5
- w_radial: float32 [8, 128], replicated, may hold values from -4 to 4
- species_embed: float32 [2, 8, 128], replicated, may hold values from -3 to 3
- w_mix: float32 [128, 128], replicated, may hold values from -0.5 to 0.5
- w_channel: float32 [2, 128, 128], replicated, may hold values from -0.5 to 0.5
- w_read: float32 [128, 128], replicated, may hold values from -0.5 to 0.5
- w_out: float32 [128], replicated, may hold values from -0.5 to 0.5
- species_energy: float32 [8], replicated, may hold values from -2 to 2
Outputs:
- atom_energy: float32 [4, 4, 2, 128], P('gx', 'gy', 'gz')
- position_grad: float32 [4, 4, 2, 3, 128], P('gx', 'gy', 'gz')
- scalar_grad: float32 [4, 4, 2, 128, 128], P('gx', 'gy', 'gz')
- vector_grad: float32 [4, 4, 2, 3, 128, 128], P('gx', 'gy', 'gz')
- weight_grad: float32 [101512], replicated
The draws below stay inside these ranges and needn't reach their ends.
Inputs may be any that keep to these rules, and one draw needn't show every extreme that they name: `atom_count`: some domain holds exactly 128 live atoms; slots at or above a domain's count are padding. `tile_counts`: entry 0 counts the live slots of the local tile (at least 512), entries 1 to 3 those of the face tiles (at least 85); some domain fills all four tiles. `local_pairs`: every slot names two different atoms of the domain, both below its atom count; live slots are those below tile_counts[0]. `face_pairs`: in tile d, entry 0 names an atom below this domain's count and entry 1 an atom below the count of the next domain along grid direction d (wrapping around); live slots are those below tile_counts[1 + d].
All inputs are finite; a program needn't handle non-finite values.
Results may differ from the reference program's by a relative error of at most 0.0003.
Values sent between devices are 32-bit elements; how exact they have to be, the bound alone decides.
A program may use at most 128 MiB of HBM per device.

```python
import jax
import jax.numpy as jnp
from jax import lax

CHANNELS = 128
BASIS = 8
SPECIES = 8
ATOMS_DEV = 128
DOM_X = 4
DOM_Y = 4
DOM_Z = 2
LOCAL_PAIRS = 1024
FACE_PAIRS = 256


def pair_tables(key):
    domain_shape = (DOM_X, DOM_Y, DOM_Z)
    domain_total = DOM_X * DOM_Y * DOM_Z
    atom_counts = jax.random.randint(jax.random.fold_in(key, 101), domain_shape, ATOMS_DEV // 2, ATOMS_DEV + 1)
    fullest = jax.random.randint(jax.random.fold_in(key, 102), (), 0, domain_total)
    marker = (jnp.arange(domain_total) == fullest).reshape(domain_shape)
    atom_counts = jnp.where(marker, ATOMS_DEV, atom_counts).astype(jnp.int32)
    local_live = jax.random.randint(jax.random.fold_in(key, 103), domain_shape, LOCAL_PAIRS // 2, LOCAL_PAIRS + 1)
    face_live = jax.random.randint(jax.random.fold_in(key, 104), domain_shape + (3,), FACE_PAIRS // 3, FACE_PAIRS + 1)
    local_live = jnp.where(marker, LOCAL_PAIRS, local_live)
    face_live = jnp.where(marker[..., None], FACE_PAIRS, face_live)
    tile_totals = jnp.concatenate([local_live[..., None], face_live], axis=-1).astype(jnp.int32)
    upper_limit = atom_counts[..., None]
    center_atoms = jax.random.randint(jax.random.fold_in(key, 105), domain_shape + (LOCAL_PAIRS,), 0, upper_limit)
    step_sizes = jax.random.randint(jax.random.fold_in(key, 106), domain_shape + (LOCAL_PAIRS,), 1, upper_limit)
    partner_atoms = (center_atoms + step_sizes) % upper_limit
    local_table = jnp.stack([center_atoms, partner_atoms], axis=3).astype(jnp.int32)
    face_tables = []
    for direction in range(3):
        neighbour_counts = jnp.roll(atom_counts, -1, axis=direction)[..., None]
        near_atoms = jax.random.randint(jax.random.fold_in(key, 107 + 2 * direction), domain_shape + (FACE_PAIRS,), 0, upper_limit)
        far_atoms = jax.random.randint(jax.random.fold_in(key, 108 + 2 * direction), domain_shape + (FACE_PAIRS,), 0, neighbour_counts)
        face_tables.append(jnp.stack([near_atoms, far_atoms], axis=3))
    face_table = jnp.stack(face_tables, axis=3).astype(jnp.int32)
    return (atom_counts, tile_totals, local_table, face_table)


def draw_atom_count(key, part):
    return pair_tables(key)[0]


def draw_tile_counts(key, part):
    return pair_tables(key)[1]


def draw_local_pairs(key, part):
    return pair_tables(key)[2]


def draw_face_pairs(key, part):
    return pair_tables(key)[3]


def set_ends(values, own_key, smallest, largest):
    longest = values.shape.index(max(values.shape))
    spots = []
    for shift in (0, 1):
        where = [jax.random.randint(jax.random.fold_in(own_key, axis), (), 0, length) for axis, length in enumerate(values.shape)]
        where[longest] = (where[longest] + shift) % values.shape[longest]
        spots.append(tuple(where))
    return values.at[spots[0]].set(smallest).at[spots[1]].set(largest)


def block_scale(key, shape, cuts, least, top_value):
    factor_of = 1.0
    for position, shards_of in cuts:
        draws = jax.random.uniform(jax.random.fold_in(jax.random.fold_in(key, 6), position), (shards_of,), jnp.float32, least / len(cuts), top_value / len(cuts))
        factor_of = factor_of * jnp.repeat(jnp.exp(draws), shape[position] // shards_of).reshape((-1,) + (1,) * (len(shape) - 1 - position))
    return factor_of


def gaussian(rng, dims, deviation, limit, pieces=(), kind=jnp.bfloat16):
    result = deviation * jax.random.normal(rng, dims, jnp.float32)
    if pieces:
        result = result * block_scale(rng, dims, pieces, -0.22, 0.18)
    return jnp.clip(result, -limit, limit).astype(kind)


def setup_inputs(seed: int = 0) -> dict:
    key_list = jax.random.split(jax.random.key(seed), 19)
    scalars = gaussian(key_list[0], (DOM_X, DOM_Y, DOM_Z, CHANNELS, ATOMS_DEV), 1.0, 6.0, ((0, 4), (1, 4), (2, 2)), jnp.float32)
    vectors = gaussian(key_list[1], (DOM_X, DOM_Y, DOM_Z, 3, CHANNELS, ATOMS_DEV), 1.0, 6.0, ((0, 4), (1, 4), (2, 2)), jnp.float32)
    positions = jnp.clip(6.0 * jax.random.uniform(key_list[2], (DOM_X, DOM_Y, DOM_Z, 3, ATOMS_DEV), jnp.float32) ** block_scale(key_list[2], (DOM_X, DOM_Y, DOM_Z, 3, ATOMS_DEV), ((0, 4), (1, 4), (2, 2)), -0.2, 0.2), 0.0, 6.0)
    species = set_ends(jax.random.randint(key_list[3], (DOM_X, DOM_Y, DOM_Z, ATOMS_DEV), 0, SPECIES), jax.random.fold_in(key_list[3], 1), 0, SPECIES - 1).astype(jnp.int32)
    atom_count = draw_atom_count(jax.random.fold_in(key_list[18], 71), 0)
    energy_weight = gaussian(key_list[5], (DOM_X, DOM_Y, DOM_Z, ATOMS_DEV), 1.0, 5.0, ((0, 4), (1, 4), (2, 2)), jnp.float32)
    local_pairs = draw_local_pairs(jax.random.fold_in(key_list[18], 71), 0)
    face_pairs = draw_face_pairs(jax.random.fold_in(key_list[18], 71), 0)
    tile_counts = draw_tile_counts(jax.random.fold_in(key_list[18], 71), 0)
    w_center = gaussian(key_list[9], (CHANNELS, CHANNELS), CHANNELS ** -0.5, 0.5, (), jnp.float32)
    w_partner = gaussian(key_list[10], (CHANNELS, CHANNELS), CHANNELS ** -0.5, 0.5, (), jnp.float32)
    w_radial = gaussian(key_list[11], (BASIS, CHANNELS), 0.8, 4.0, (), jnp.float32)
    species_embed = gaussian(key_list[12], (2, SPECIES, CHANNELS), 0.6, 3.0, (), jnp.float32)
    w_mix = gaussian(key_list[13], (CHANNELS, CHANNELS), CHANNELS ** -0.5, 0.5, (), jnp.float32)
    w_channel = gaussian(key_list[14], (2, CHANNELS, CHANNELS), CHANNELS ** -0.5, 0.5, (), jnp.float32)
    w_read = gaussian(key_list[15], (CHANNELS, CHANNELS), CHANNELS ** -0.5, 0.5, (), jnp.float32)
    w_out = gaussian(key_list[16], (CHANNELS,), CHANNELS ** -0.5, 0.5, (), jnp.float32)
    species_energy = jnp.clip(jax.random.uniform(key_list[17], (SPECIES,), jnp.float32, -2.0, 2.0), -2.0, 2.0)
    return dict(scalars=scalars, vectors=vectors, positions=positions, species=species, atom_count=atom_count, energy_weight=energy_weight, local_pairs=local_pairs, face_pairs=face_pairs, tile_counts=tile_counts, w_center=w_center, w_partner=w_partner, w_radial=w_radial, species_embed=species_embed, w_mix=w_mix, w_channel=w_channel, w_read=w_read, w_out=w_out, species_energy=species_energy)


cutoff_radius = 5.0
cell_edge = 6.0
highest = lax.Precision.HIGHEST

def edge_energy(edge_params, center_proj, partner_proj, center_vecs, partner_vecs, displace):
    radial_weight, mix_weight, channel_weight, read_weight, out_weight = edge_params
    squared = lax.optimization_barrier(jnp.sum(displace * displace, axis=0))
    basis_count = radial_weight.shape[0]
    spacing = cutoff_radius * cutoff_radius / (basis_count - 1)
    centers_sq = spacing * jnp.arange(basis_count).astype(jnp.float32)
    radial_basis = jnp.exp(-jnp.square((squared[None, :] - centers_sq[:, None]) / spacing))
    latent_in = center_proj + partner_proj + jnp.dot(radial_weight.T, radial_basis, precision=highest)
    first_hidden = jax.nn.silu(latent_in)
    second = first_hidden + jax.nn.silu(jnp.dot(mix_weight.T, first_hidden, precision=highest))
    vector_gain = jnp.dot(channel_weight[0].T, second, precision=highest)
    tensor_gain = jnp.dot(channel_weight[1].T, second, precision=highest)
    bond_vector = displace / cutoff_radius
    along_partner = lax.optimization_barrier(jnp.sum(bond_vector[:, None, :] * partner_vecs, axis=0))
    along_center = lax.optimization_barrier(jnp.sum(bond_vector[:, None, :] * center_vecs, axis=0))
    inner_product = lax.optimization_barrier(jnp.sum(center_vecs * partner_vecs, axis=0))
    scaled_sq = squared / (cutoff_radius * cutoff_radius)
    quadratic = along_center * along_partner - scaled_sq[None, :] * inner_product / 3.0
    mixed_latent = second + vector_gain * along_partner + tensor_gain * quadratic
    readout = jnp.dot(out_weight, jax.nn.silu(jnp.dot(read_weight.T, mixed_latent, precision=highest)), precision=highest)
    envelope = 1.0 / (1.0 + scaled_sq)
    return envelope * readout

def tile_loss(edge_params, center, partner, center_weight, partner_weight, pair_list, live_count, offset):
    center_proj, center_vecs, center_coords = center
    partner_proj, partner_vecs, partner_coords = partner
    center_rows = pair_list[0]
    partner_rows = pair_list[1]
    slot_count = pair_list.shape[1]
    live_mask = (jnp.arange(slot_count, dtype=jnp.int32) < live_count).astype(jnp.float32)
    displace = jnp.take(partner_coords, partner_rows, axis=1) + offset[:, None] - jnp.take(center_coords, center_rows, axis=1)
    energies = edge_energy(edge_params, jnp.take(center_proj, center_rows, axis=1), jnp.take(partner_proj, partner_rows, axis=1), jnp.take(center_vecs, center_rows, axis=2), jnp.take(partner_vecs, partner_rows, axis=2), displace)
    halves = 0.5 * live_mask * energies
    weighted_sum = jnp.sum(halves * (center_weight[center_rows] + partner_weight[partner_rows]))
    center_energy = jnp.zeros((center_proj.shape[1],), jnp.float32).at[center_rows].add(halves)
    partner_energy = jnp.zeros((partner_proj.shape[1],), jnp.float32).at[partner_rows].add(halves)
    return (weighted_sum, (center_energy, partner_energy))

def face_offset(direction):
    return cell_edge * (jnp.arange(3) == direction).astype(jnp.float32)

def domain_step(edge_params, domain_item):
    center_here, partner_here, vecs_here, coords_here, weights_here, local_list, face_list, live_counts, near_proj, near_vecs, near_coords, near_weights = domain_item
    center = (center_here, vecs_here, coords_here)
    weighted_sum, (center_energy, partner_energy) = tile_loss(edge_params, center, (partner_here, vecs_here, coords_here), weights_here, weights_here, local_list, live_counts[0], jnp.zeros((3,), jnp.float32))
    pair_energy = center_energy + partner_energy
    returned = []
    for direction in range(3):
        face_sum, (center_face, partner_face) = tile_loss(edge_params, center, (near_proj[direction], near_vecs[direction], near_coords[direction]), weights_here, near_weights[direction], face_list[direction], live_counts[direction + 1], face_offset(direction))
        weighted_sum = weighted_sum + face_sum
        pair_energy = pair_energy + center_face
        returned.append(partner_face)
    return (weighted_sum, pair_energy, jnp.stack(returned, axis=0))

def reference(scalars, vectors, positions, species, atom_count, energy_weight, local_pairs, face_pairs, tile_counts, w_center, w_partner, w_radial, species_embed, w_mix, w_channel, w_read, w_out, species_energy):
    grid_shape = scalars.shape[:3]
    domain_total = grid_shape[0] * grid_shape[1] * grid_shape[2]
    atom_slots = scalars.shape[4]
    kind_count = species_energy.shape[0]
    species_hot = (species[..., None, :] == jnp.arange(kind_count, dtype=jnp.int32)[:, None]).astype(jnp.float32)
    valid_atoms = (jnp.arange(atom_slots, dtype=jnp.int32) < atom_count[..., None]).astype(jnp.float32)

    def flat_domains(array):
        return array.reshape((domain_total,) + array.shape[3:])

    def neighbours(array):
        return flat_domains(jnp.stack([jnp.roll(array, -1, axis=direction) for direction in range(3)], axis=3))
    checked_step = jax.checkpoint(domain_step)

    def total_loss(center_matrix, partner_matrix, radial_matrix, embed_table, mix_matrix, channel_matrix, read_matrix, out_vector, reference_energy, scalar_in, vector_in, coords_in):
        center_proj = jnp.einsum('dc,xyzda->xyzca', center_matrix, scalar_in, precision=highest) + jnp.einsum('sc,xyzsa->xyzca', embed_table[0], species_hot, precision=highest)
        partner_proj = jnp.einsum('dc,xyzda->xyzca', partner_matrix, scalar_in, precision=highest) + jnp.einsum('sc,xyzsa->xyzca', embed_table[1], species_hot, precision=highest)
        self_energy = valid_atoms * jnp.einsum('s,xyzsa->xyza', reference_energy, species_hot, precision=highest)
        edge_params = (radial_matrix, mix_matrix, channel_matrix, read_matrix, out_vector)
        domain_items = (flat_domains(center_proj), flat_domains(partner_proj), flat_domains(vector_in), flat_domains(coords_in), flat_domains(energy_weight), flat_domains(local_pairs), flat_domains(face_pairs), flat_domains(tile_counts), neighbours(partner_proj), neighbours(vector_in), neighbours(coords_in), neighbours(energy_weight))
        losses, pair_energy, returned = lax.map(lambda domain_item: checked_step(edge_params, domain_item), domain_items)
        pair_energy = pair_energy.reshape(grid_shape + (atom_slots,))
        returned = returned.reshape(grid_shape + (3, atom_slots))
        for direction in range(3):
            pair_energy = pair_energy + jnp.roll(returned[..., direction, :], 1, axis=direction)
        atom_energy = self_energy + pair_energy
        return (jnp.sum(losses) + jnp.sum(energy_weight * self_energy), atom_energy)
    primal, pull_back, atom_energy = jax.vjp(total_loss, w_center, w_partner, w_radial, species_embed, w_mix, w_channel, w_read, w_out, species_energy, scalars, vectors, positions, has_aux=True)
    grads = pull_back(jnp.ones_like(primal))
    weight_grad = jnp.concatenate([piece_grad.reshape(-1) for piece_grad in grads[:9]]) / domain_total
    return (atom_energy, grads[11], grads[9], grads[10], weight_grad)
```

```python
import functools

import jax
import jax.numpy as jnp
from jax import lax
from jax.experimental import pallas as pl
from jax.experimental.pallas import tpu as pltpu
from jax.sharding import PartitionSpec as P

CUTOFF = 5.0
EDGE = 6.0
HIGHEST = lax.Precision.HIGHEST
F32 = jnp.float32
B16 = jnp.bfloat16
AXES = ("gx", "gy", "gz")
MESH = pl.DeviceIdType.MESH
ORDER = (1, 2, 0)


def split(x):
    hi = x.astype(B16)
    return hi, (x - hi.astype(F32)).astype(B16)


def weight3(w):
    hi, lo = split(w)
    return jnp.concatenate([hi, hi, lo], axis=1)


def stack3(pair):
    return jnp.concatenate([pair[0], pair[1], pair[0]], axis=0)


def mul(a, b):
    return jnp.dot(a, b, preferred_element_type=F32)


def mul_t(a, b, precision=None):
    return lax.dot_general(
        a, b, (((1,), (1,)), ((), ())), precision=precision, preferred_element_type=F32
    )


def outer3(x, g):
    left = jnp.concatenate([x[0], x[1], x[0]], axis=1)
    right = jnp.concatenate([g[0], g[0], g[1]], axis=1)
    return mul_t(left, right)


def gate(x):
    return 0.5 * jnp.tanh(0.5 * x) + 0.5


def rows_of(parts, count, width):
    row = lax.broadcasted_iota(jnp.int32, (count, width), 0)
    total = jnp.zeros((count, width), F32)
    for k, part in enumerate(parts):
        total = jnp.where(row == k, part, total)
    return total


def phase_list(sizes):
    nx, ny, nz = sizes
    phases = []
    if nx % 2 == 0 and nx > 2:
        phases += [("gx", 1, 2), ("gx", 2, nx // 2)]
    else:
        phases += [("gx", 1, nx)]
    phases += [("gz", 1, nz), ("gy", 1, ny)]
    return [p for p in phases if p[2] > 1]


def kernel(sizes, rows, block_pairs, *refs):
    phases = phase_list(sizes)
    n_phases = len(phases)
    (sc, vec, small, lp, fp, counts, atoms, wc, wp, wr, emb, wmix, wch, wread, wout, ref_e,
     energy_out, pos_out, sgrad_out, vgrad_out, wgrad_out,
     here, there, near, ret, back, acc_c, acc_p, gbuf, agb,
     mix_f, mix_b, ch_f, ch_b, read_f, read_b) = refs[:36]
    landing = refs[36:36 + n_phases]
    in_send, in_recv, ret_send, ret_recv, rs_send, rs_recv, ag_send, ag_recv = refs[36 + n_phases:]
    atom_slots = sc.shape[1]
    channels = sc.shape[0]
    species_count = wr.shape[0]
    index = {a: lax.axis_index(a) for a in AXES}

    def neighbour(d, step):
        n = sizes[d]
        return {AXES[d]: lax.rem(index[AXES[d]] + step + n, n)}

    def peer(phase, k):
        axis, stride, size = phase
        q = lax.rem(index[axis] // stride, size)
        t = lax.rem(q + k, size)
        return q, t, {axis: index[axis] + (t - q) * stride}

    greeted = []
    for d in range(3):
        greeted.append(neighbour(d, 1))
        if sizes[d] > 2:
            greeted.append(neighbour(d, -1))
    for phase in phases:
        for k in range(1, phase[2]):
            greeted.append(peer(phase, k)[2])
    barrier = pltpu.get_barrier_semaphore()
    for target in greeted:
        pl.semaphore_signal(barrier, inc=1, device_id=target, device_id_type=MESH)
    pl.semaphore_wait(barrier, len(greeted))

    inbound = {}
    for d in ORDER:
        copies = []
        for part, (src, lo, hi) in enumerate(((small, 512, 520), (sc, 0, 128), (vec, 128, 512))):
            copy = pltpu.make_async_remote_copy(
                src_ref=src,
                dst_ref=near.at[d, lo:hi],
                send_sem=in_send.at[3 * d + part],
                recv_sem=in_recv.at[3 * d + part],
                device_id=neighbour(d, -1),
                device_id_type=MESH,
            )
            copy.start()
            copies.append(copy)
        inbound[d] = copies

    mix_b[...] = weight3(wmix[...])
    mix_f[...] = weight3(wmix[...].T)
    read_b[...] = weight3(wread[...])
    read_f[...] = weight3(wread[...].T)
    ch_b[...] = weight3(jnp.concatenate([wch[0:128], wch[128:256]], axis=1))
    ch_f[...] = weight3(jnp.concatenate([wch[0:128].T, wch[128:256].T], axis=0))
    radial = wr[...]
    radial_t = jnp.concatenate([radial] * (channels // species_count), axis=0).T[:, 0:species_count]
    out_col = jnp.broadcast_to(wout[...], (channels, channels)).T[:, 0:1]
    wc_t = weight3(wc[...].T)
    wp_t = weight3(wp[...].T)
    gbuf[...] = jnp.zeros_like(gbuf)
    acc_c[...] = jnp.zeros_like(acc_c)
    acc_p[...] = jnp.zeros_like(acc_p)

    def hot_of(small_rows):
        row = lax.broadcasted_iota(jnp.int32, (species_count, atom_slots), 0).astype(F32)
        return (row == small_rows[4:5]).astype(F32)

    def embed(table, hot):
        return lax.dot_general(
            table, hot, (((0,), (0,)), ((), ())), precision=HIGHEST, preferred_element_type=F32
        )

    def fill(dst, proj, vectors, small_rows):
        hi, lo = split(proj)
        dst[0:128, 0:128] = hi
        dst[0:128, 128:256] = lo
        hi, lo = split(vectors)
        dst[128:512, 0:128] = hi
        dst[128:512, 128:256] = lo
        hi, lo = split(small_rows)
        hi, lo = hi.astype(F32), lo.astype(F32)
        rest = small_rows - hi - lo
        top = jnp.concatenate([hi, lo], axis=1)
        low = jnp.concatenate([rest, jnp.zeros_like(rest)], axis=1)
        dst[512:528, :] = jnp.concatenate([top, low], axis=0).astype(B16)

    hot = hot_of(small)
    sc3 = stack3(split(sc[...]))
    fill(here, mul(wc_t, sc3) + embed(emb[0:8], hot), vec[...], small[...])
    fill(there, mul(wp_t, sc3) + embed(emb[8:16], hot), vec[...], small[...])

    width = block_pairs
    spacing = CUTOFF * CUTOFF / (species_count - 1)

    def block(ii, jj, live, offsets):
        lane_atoms = lax.broadcasted_iota(jnp.int32, (atom_slots, width), 0)
        oi = (lane_atoms == ii).astype(F32).astype(B16)
        oj = (lane_atoms == jj).astype(F32).astype(B16)
        at_i = mul(here[...], jnp.concatenate([oi, oi], axis=0))
        at_j = mul(there[...], jnp.concatenate([oj, oj], axis=0))
        si = at_i[512:520] + at_i[520:528]
        sj = at_j[512:520] + at_j[520:528]
        cv = [at_i[128 * (k + 1):128 * (k + 2)] for k in range(3)]
        pv = [at_j[128 * (k + 1):128 * (k + 2)] for k in range(3)]
        d = [sj[k:k + 1] + offsets[k] - si[k:k + 1] for k in range(3)]
        pair_weight = si[3:4] + sj[3:4]
        sq = d[0] * d[0] + d[1] * d[1] + d[2] * d[2]
        order = lax.broadcasted_iota(jnp.int32, (species_count, width), 0).astype(F32)
        t = (sq - order * spacing) / spacing
        basis = jnp.exp(-(t * t))
        latent = at_i[0:128] + at_j[0:128] + jnp.dot(
            radial_t, basis, precision=HIGHEST, preferred_element_type=F32
        )
        s1 = gate(latent)
        first = latent * s1
        first2 = split(first)
        m = mul(mix_f[...], stack3(first2))
        s2 = gate(m)
        second = first + m * s2
        second2 = split(second)
        gains = mul(ch_f[...], stack3(second2))
        vg, tg = gains[0:128], gains[128:256]
        n = [x * (1.0 / CUTOFF) for x in d]
        ap = n[0] * pv[0] + n[1] * pv[1] + n[2] * pv[2]
        ac = n[0] * cv[0] + n[1] * cv[1] + n[2] * cv[2]
        ip = cv[0] * pv[0] + cv[1] * pv[1] + cv[2] * pv[2]
        ss = sq * (1.0 / (CUTOFF * CUTOFF))
        third = ss * (1.0 / 3.0)
        q = ac * ap - third * ip
        mixed = second + vg * ap + tg * q
        mixed2 = split(mixed)
        u = mul(read_f[...], stack3(mixed2))
        s3 = gate(u)
        h = u * s3
        readout = jnp.sum(out_col * h, axis=0, keepdims=True)
        env = 1.0 / (1.0 + ss)
        half_live = 0.5 * live
        halves = half_live * env * readout
        ge = half_live * pair_weight
        gr = ge * env
        gbuf[792:800] += mul_t(rows_of([gr], 8, width), h, HIGHEST)
        du = (out_col * gr) * (s3 * (1.0 + u * (1.0 - s3)))
        du2 = split(du)
        gbuf[664:792] += outer3(mixed2, du2)
        dmixed = mul(read_b[...], stack3(du2))
        dq = dmixed * tg
        dap = dmixed * vg + dq * ac
        dac = dq * ap
        dip = -third * dq
        dss = -jnp.sum(dq * ip, axis=0, keepdims=True) * (1.0 / 3.0)
        dgain2 = split(jnp.concatenate([dmixed * ap, dmixed * q], axis=0))
        dch = outer3(second2, dgain2)
        gbuf[408:536] += dch[:, 0:128]
        gbuf[536:664] += dch[:, 128:256]
        dsecond = dmixed + mul(ch_b[...], stack3(dgain2))
        dm = dsecond * (s2 * (1.0 + m * (1.0 - s2)))
        dm2 = split(dm)
        gbuf[280:408] += outer3(first2, dm2)
        dfirst = dsecond + mul(mix_b[...], stack3(dm2))
        dlat = dfirst * (s1 * (1.0 + latent * (1.0 - s1)))
        gbuf[256:264] += mul_t(basis, dlat, HIGHEST)
        dbasis = jnp.dot(radial, dlat, precision=HIGHEST, preferred_element_type=F32)
        dsq = jnp.sum(dbasis * basis * t, axis=0, keepdims=True) * (-2.0 / spacing)
        dsq = dsq + (dss - ge * readout * env * env) * (1.0 / (CUTOFF * CUTOFF))
        dcv = [n[k] * dac + dip * pv[k] for k in range(3)]
        dpv = [n[k] * dap + dip * cv[k] for k in range(3)]
        dd = [
            jnp.sum(dac * cv[k] + dap * pv[k], axis=0, keepdims=True) * (1.0 / CUTOFF)
            + 2.0 * d[k] * dsq
            for k in range(3)
        ]
        lat2 = split(dlat)

        def scatter(vector_parts, small_parts, one_hot):
            pieces = [lat2] + [split(v) for v in vector_parts]
            pieces.append(split(rows_of(small_parts, 16, width)))
            his = jnp.concatenate([p[0] for p in pieces], axis=0)
            los = jnp.concatenate([p[1] for p in pieces], axis=0)
            return mul_t(
                jnp.concatenate([his, los], axis=1), jnp.concatenate([one_hot, one_hot], axis=1)
            )

        acc_c[...] += scatter(dcv, [-dd[0], -dd[1], -dd[2], halves], oi)
        return scatter(dpv, dd + [halves], oj)

    slot = lax.broadcasted_iota(jnp.int32, (1, width), 1)

    def local_step(step, carry):
        start = pl.multiple_of(step * width, width)
        pairs = lp[:, pl.ds(start, width)]
        live = (slot + start < counts[0]).astype(F32)
        acc_p[...] += block(pairs[0:1], pairs[1:2], live, (0.0, 0.0, 0.0))
        return carry

    lax.fori_loop(0, lp.shape[1] // width, local_step, 0)

    sc2 = split(sc[...])
    gbuf[128:256] += outer3(sc2, split(acc_p[0:128]))
    gbuf[272:280] += mul_t(hot, acc_p[0:128], HIGHEST)

    returning = []
    for d in ORDER:
        for copy in inbound[d]:
            copy.wait()
        near_hot = hot_of(near[d, 512:520])
        near2 = split(near[d, 0:128])
        fill(there, mul(wp_t, stack3(near2)) + embed(emb[8:16], near_hot),
             near[d, 128:512], near[d, 512:520])
        live = (slot < counts[1 + d]).astype(F32)
        offsets = tuple(EDGE if k == d else 0.0 for k in range(3))
        ret[d] = block(fp[2 * d:2 * d + 1], fp[2 * d + 1:2 * d + 2], live, offsets)
        copy = pltpu.make_async_remote_copy(
            src_ref=ret.at[d, 0:520],
            dst_ref=back.at[d],
            send_sem=ret_send.at[d],
            recv_sem=ret_recv.at[d],
            device_id=neighbour(d, 1),
            device_id_type=MESH,
        )
        copy.start()
        returning.append(copy)
        proj_grad = ret[d, 0:128]
        gbuf[128:256] += outer3(near2, split(proj_grad))
        gbuf[272:280] += mul_t(near_hot, proj_grad, HIGHEST)

    center_grad = acc_c[0:128]
    gbuf[0:128] += outer3(sc2, split(center_grad))
    gbuf[264:272] += mul_t(hot, center_grad, HIGHEST)
    lane = lax.broadcasted_iota(jnp.int32, (1, atom_slots), 1)
    valid = (lane < atoms[0]).astype(F32)
    weighted = small[3:4] * valid
    wide_hot = (
        lax.broadcasted_iota(jnp.int32, (atom_slots, atom_slots), 0).astype(F32) == small[4:5]
    ).astype(F32)
    gbuf[792:800] += mul_t(
        rows_of([jnp.zeros_like(weighted), weighted], 8, atom_slots), wide_hot, HIGHEST
    )

    def finish():
        for copy in returning:
            copy.wait()
        vgrad_out[...] = acc_c[128:512] + acc_p[128:512] + (
            back[0, 128:512] + back[1, 128:512] + back[2, 128:512]
        )
        tail = acc_c[512:520] + acc_p[512:520] + (
            back[0, 512:520] + back[1, 512:520] + back[2, 512:520]
        )
        pos_out[...] = tail[0:3]
        self_energy = jnp.zeros((1, atom_slots), F32)
        for s in range(species_count):
            self_energy = self_energy + jnp.where(small[4:5] == float(s), ref_e[s], 0.0)
        energy_out[...] = tail[3:4] + valid * self_energy
        partner = acc_p[0:128] + (back[0, 0:128] + back[1, 0:128] + back[2, 0:128])
        sgrad_out[...] = mul(weight3(wc[...]), stack3(split(acc_c[0:128]))) + mul(
            weight3(wp[...]), stack3(split(partner))
        )

    start, length, sem = 0, rows, 0
    held = []
    for p, phase in enumerate(phases):
        size = phase[2]
        chunk = length // size
        copies = []
        for k in range(1, size):
            q, t, target = peer(phase, k)
            copy = pltpu.make_async_remote_copy(
                src_ref=gbuf.at[pl.ds(pl.multiple_of(start + t * chunk, 8), chunk)],
                dst_ref=landing[p].at[k - 1],
                send_sem=rs_send.at[sem],
                recv_sem=rs_recv.at[sem],
                device_id=target,
                device_id_type=MESH,
            )
            copy.start()
            copies.append(copy)
            sem += 1
        q = peer(phase, 0)[0]
        start = start + q * chunk
        mine = pl.ds(pl.multiple_of(start, 8), chunk)
        if p == min(1, n_phases - 1):
            finish()
        for copy in copies:
            copy.wait()
        total = gbuf[mine, :]
        for k in range(size - 1):
            total = total + landing[p][k]
        if p == n_phases - 1:
            agb[mine, :] = total * (1.0 / (sizes[0] * sizes[1] * sizes[2]))
        else:
            gbuf[mine, :] = total
        held.append((phase, start, chunk))
        length = chunk
    sem = 0
    for phase, start, chunk in reversed(held):
        mine = pl.ds(pl.multiple_of(start, 8), chunk)
        copies = []
        for k in range(1, phase[2]):
            copy = pltpu.make_async_remote_copy(
                src_ref=agb.at[mine],
                dst_ref=agb.at[mine],
                send_sem=ag_send.at[sem],
                recv_sem=ag_recv.at[sem],
                device_id=peer(phase, k)[2],
                device_id_type=MESH,
            )
            copy.start()
            copies.append(copy)
            sem += 1
        for copy in copies:
            copy.wait()
    wgrad_out[...] = agb[0:800]


def per_device(scalars, vectors, positions, species, atom_count, energy_weight, local_pairs,
               face_pairs, tile_counts, w_center, w_partner, w_radial, species_embed, w_mix,
               w_channel, w_read, w_out, species_energy, *, sizes):
    channels, atom_slots = scalars.shape[3:]
    small = jnp.concatenate(
        [
            positions[0, 0, 0],
            energy_weight[0, 0],
            species[0, 0].astype(F32),
            jnp.zeros((3, atom_slots), F32),
        ],
        axis=0,
    )
    width = face_pairs.shape[-1]
    total = sizes[0] * sizes[1] * sizes[2]
    rows = -(-800 // (8 * total)) * 8 * total
    phases = phase_list(sizes)
    landing, length, n_sems = [], rows, 0
    for _, _, size in phases:
        length //= size
        landing.append(pltpu.VMEM((size - 1, length, 128), F32))
        n_sems += size - 1
    vmem = pl.BlockSpec(memory_space=pltpu.VMEM)
    smem = pl.BlockSpec(memory_space=pltpu.SMEM)
    dma = pltpu.SemaphoreType.DMA
    energy, pos, sgrad, vgrad, wgrad = pl.pallas_call(
        functools.partial(kernel, sizes, rows, width),
        out_shape=(
            jax.ShapeDtypeStruct((1, atom_slots), F32),
            jax.ShapeDtypeStruct((3, atom_slots), F32),
            jax.ShapeDtypeStruct((channels, atom_slots), F32),
            jax.ShapeDtypeStruct((3 * channels, atom_slots), F32),
            jax.ShapeDtypeStruct((800, 128), F32),
        ),
        in_specs=[vmem] * 5 + [smem] * 2 + [vmem] * 8 + [smem],
        out_specs=(vmem,) * 5,
        scratch_shapes=[
            pltpu.VMEM((528, 256), B16),
            pltpu.VMEM((528, 256), B16),
            pltpu.VMEM((3, 520, 128), F32),
            pltpu.VMEM((3, 528, 128), F32),
            pltpu.VMEM((3, 520, 128), F32),
            pltpu.VMEM((528, 128), F32),
            pltpu.VMEM((528, 128), F32),
            pltpu.VMEM((rows, 128), F32),
            pltpu.VMEM((rows, 128), F32),
            pltpu.VMEM((128, 384), B16),
            pltpu.VMEM((128, 384), B16),
            pltpu.VMEM((256, 384), B16),
            pltpu.VMEM((128, 768), B16),
            pltpu.VMEM((128, 384), B16),
            pltpu.VMEM((128, 384), B16),
        ] + landing + [
            dma((9,)), dma((9,)), dma((3,)), dma((3,)),
            dma((n_sems,)), dma((n_sems,)), dma((n_sems,)), dma((n_sems,)),
        ],
        compiler_params=pltpu.CompilerParams(
            collective_id=0, has_side_effects=True, vmem_limit_bytes=40 * 1024 * 1024
        ),
    )(
        scalars[0, 0, 0],
        vectors[0, 0, 0].reshape(3 * channels, atom_slots),
        small,
        local_pairs[0, 0, 0],
        face_pairs[0, 0, 0].reshape(6, width),
        tile_counts[0, 0, 0],
        atom_count[0, 0],
        w_center,
        w_partner,
        w_radial,
        species_embed.reshape(-1, channels),
        w_mix,
        w_channel.reshape(-1, channels),
        w_read,
        w_out[None, :],
        species_energy,
    )
    weight_count = sum(
        w.size for w in (w_center, w_partner, w_radial, species_embed, w_mix, w_channel, w_read,
                         w_out, species_energy)
    )
    return (
        energy[None, None],
        pos[None, None, None],
        sgrad[None, None, None],
        vgrad.reshape(3, channels, atom_slots)[None, None, None],
        wgrad.reshape(-1)[:weight_count],
    )


def solution(mesh):
    sizes = tuple(mesh.shape[a] for a in AXES)
    here = ("gx", "gy", "gz")
    return jax.shard_map(
        functools.partial(per_device, sizes=sizes),
        mesh=mesh,
        in_specs=(
            P(*here, None, None),
            P(*here, None, None, None),
            P(*here, None, None),
            P(*here, None),
            P(*here),
            P(*here, None),
            P(*here, None, None),
            P(*here, None, None, None),
            P(*here, None),
        ) + (P(),) * 9,
        out_specs=(
            P(*here, None),
            P(*here, None, None),
            P(*here, None, None),
            P(*here, None, None, None),
            P(),
        ),
        check_vma=False,
    )
```

```python
import functools

import jax
import jax.numpy as jnp
from jax import lax
from jax.experimental import pallas as pl
from jax.experimental.pallas import tpu as pltpu
from jax.sharding import PartitionSpec as P

CUTOFF = 5.0
EDGE = 6.0
HIGHEST = lax.Precision.HIGHEST
F32 = jnp.float32
B16 = jnp.bfloat16
AXES = ("gx", "gy", "gz")
MESH = pl.DeviceIdType.MESH
ORDER = (1, 2, 0)


def split(x):
    hi = x.astype(B16)
    return hi, (x - hi.astype(F32)).astype(B16)


def weight3(w):
    hi, lo = split(w)
    return jnp.concatenate([hi, hi, lo], axis=1)


def stack3(pair):
    return jnp.concatenate([pair[0], pair[1], pair[0]], axis=0)


def mul(a, b):
    return jnp.dot(a, b, preferred_element_type=F32)


def mul_t(a, b, precision=None):
    return lax.dot_general(
        a, b, (((1,), (1,)), ((), ())), precision=precision, preferred_element_type=F32
    )


def outer3(x, g):
    left = jnp.concatenate([x[0], x[1], x[0]], axis=1)
    right = jnp.concatenate([g[0], g[0], g[1]], axis=1)
    return mul_t(left, right)


def gate(x):
    return 0.5 * jnp.tanh(0.5 * x) + 0.5


def rows_of(parts, count, width):
    row = lax.broadcasted_iota(jnp.int32, (count, width), 0)
    total = jnp.zeros((count, width), F32)
    for k, part in enumerate(parts):
        total = jnp.where(row == k, part, total)
    return total


def phase_list(sizes):
    nx, ny, nz = sizes
    phases = []
    if nx % 2 == 0 and nx > 2:
        phases += [("gx", 1, 2), ("gx", 2, nx // 2)]
    else:
        phases += [("gx", 1, nx)]
    phases += [("gz", 1, nz), ("gy", 1, ny)]
    return [p for p in phases if p[2] > 1]


def kernel(sizes, rows, block_pairs, *refs):
    phases = phase_list(sizes)
    n_phases = len(phases)
    (sc_h, vec_h, pos_h, weight_h, kind_h, lp_h, fp_h, counts, atoms, wc_h, wp_h, wr, emb, wmix_h, wch_h, wread_h,
     wout, ref_e, energy_out, pos_out, sgrad_out, vgrad_out, wgrad_out,
     here, there, near, ret, back, acc_c, acc_p, gbuf, agb,
     mix_f, mix_b, ch_f, ch_b, read_f, read_b,
     sc, vec, lp, fp, wc, wp, wmix, wch, wread, acc_out, acc_rad, small, pos_v, weight_v, kind_v) = refs[:53]
    landing = refs[53:53 + n_phases]
    (in_send, in_recv, ret_send, ret_recv, rs_send, rs_recv, ag_send, ag_recv,
     load_sem) = refs[53 + n_phases:]
    loads = []
    for k, (src, dst) in enumerate(
        ((pos_h, pos_v), (weight_h, weight_v), (kind_h, kind_v), (sc_h, sc), (wc_h, wc), (wp_h, wp), (vec_h, vec), (lp_h, lp), (wmix_h, wmix),
         (wch_h, wch), (wread_h, wread), (fp_h, fp))
    ):
        copy = pltpu.make_async_copy(src, dst, load_sem.at[k])
        copy.start()
        loads.append(copy)
    atom_slots = sc.shape[1]
    channels = sc.shape[0]
    species_count = wr.shape[0]
    index = {a: lax.axis_index(a) for a in AXES}

    def neighbour(d, step):
        n = sizes[d]
        return {AXES[d]: lax.rem(index[AXES[d]] + step + n, n)}

    def peer(phase, k):
        axis, stride, size = phase
        q = lax.rem(index[axis] // stride, size)
        t = lax.rem(q + k, size)
        return q, t, {axis: index[axis] + (t - q) * stride}

    greeted = []
    for d in range(3):
        greeted.append(neighbour(d, 1))
        if sizes[d] > 2:
            greeted.append(neighbour(d, -1))
    for phase in phases:
        for k in range(1, phase[2]):
            greeted.append(peer(phase, k)[2])
    barrier = pltpu.get_barrier_semaphore()
    for target in greeted:
        pl.semaphore_signal(barrier, inc=1, device_id=target, device_id_type=MESH)
    pl.semaphore_wait(barrier, len(greeted))

    for copy in loads[:3]:
        copy.wait()
    coords = pos_v[...]
    small[...] = rows_of(
        [coords[0:1], coords[1:2], coords[2:3], weight_v[...], kind_v[...].astype(F32)],
        8, atom_slots,
    )
    inbound = {}
    for d in ORDER:
        copies = []
        for part, (src, lo, hi) in enumerate(((small, 512, 520), (sc_h, 0, 128), (vec_h, 128, 512))):
            copy = pltpu.make_async_remote_copy(
                src_ref=src,
                dst_ref=near.at[d, lo:hi],
                send_sem=in_send.at[3 * d + part],
                recv_sem=in_recv.at[3 * d + part],
                device_id=neighbour(d, -1),
                device_id_type=MESH,
            )
            copy.start()
            copies.append(copy)
        inbound[d] = copies

    for copy in loads[3:]:
        copy.wait()
    mix_b[...] = weight3(wmix[...])
    mix_f[...] = weight3(wmix[...].T)
    read_b[...] = weight3(wread[...])
    read_f[...] = weight3(wread[...].T)
    ch_b[...] = weight3(jnp.concatenate([wch[0:128], wch[128:256]], axis=1))
    ch_f[...] = weight3(jnp.concatenate([wch[0:128].T, wch[128:256].T], axis=0))
    radial = wr[...]
    rad_hi = radial.astype(B16).astype(F32)
    rad_lo = (radial - rad_hi).astype(B16).astype(F32)
    rad_zero = jnp.zeros_like(radial)
    radial_t = jnp.concatenate(
        [rad_hi, rad_hi, rad_lo] + [rad_zero] * (channels // species_count - 3), axis=0
    ).T[:, 0:4 * species_count].astype(B16)
    radial_b = weight3(jnp.concatenate([radial, rad_zero], axis=0))
    out_col = jnp.broadcast_to(wout[...], (channels, channels)).T[:, 0:1]
    wc_t = weight3(wc[...].T)
    wp_t = weight3(wp[...].T)
    gbuf[...] = jnp.zeros_like(gbuf)
    acc_c[...] = jnp.zeros_like(acc_c)
    acc_p[...] = jnp.zeros_like(acc_p)
    acc_out[...] = jnp.zeros_like(acc_out)
    acc_rad[...] = jnp.zeros_like(acc_rad)

    def hot_of(small_rows):
        row = lax.broadcasted_iota(jnp.int32, (species_count, atom_slots), 0).astype(F32)
        return (row == small_rows[4:5]).astype(F32)

    def embed(table, hot):
        return lax.dot_general(
            table, hot, (((0,), (0,)), ((), ())), precision=HIGHEST, preferred_element_type=F32
        )

    def fill(dst, proj, vectors, small_rows):
        hi, lo = split(proj)
        dst[0:128, 0:128] = hi
        dst[0:128, 128:256] = lo
        hi, lo = split(vectors)
        dst[128:512, 0:128] = hi
        dst[128:512, 128:256] = lo
        hi, lo = split(small_rows)
        hi, lo = hi.astype(F32), lo.astype(F32)
        rest = small_rows - hi - lo
        top = jnp.concatenate([hi, lo], axis=1)
        low = jnp.concatenate([rest, jnp.zeros_like(rest)], axis=1)
        dst[512:528, :] = jnp.concatenate([top, low], axis=0).astype(B16)

    hot = hot_of(small)
    sc3 = stack3(split(sc[...]))
    fill(here, mul(wc_t, sc3) + embed(emb[0:8], hot), vec[...], small[...])
    fill(there, mul(wp_t, sc3) + embed(emb[8:16], hot), vec[...], small[...])

    width = block_pairs
    spacing = CUTOFF * CUTOFF / (species_count - 1)

    def block(ii, jj, live, offsets):
        lane_atoms = lax.broadcasted_iota(jnp.int32, (atom_slots, width), 0)
        oi = (lane_atoms == ii).astype(F32).astype(B16)
        oj = (lane_atoms == jj).astype(F32).astype(B16)
        at_i = mul(here[...], jnp.concatenate([oi, oi], axis=0))
        at_j = mul(there[...], jnp.concatenate([oj, oj], axis=0))
        si = at_i[512:520] + at_i[520:528]
        sj = at_j[512:520] + at_j[520:528]
        cv = [at_i[128 * (k + 1):128 * (k + 2)] for k in range(3)]
        pv = [at_j[128 * (k + 1):128 * (k + 2)] for k in range(3)]
        d = [sj[k:k + 1] + offsets[k] - si[k:k + 1] for k in range(3)]
        pair_weight = si[3:4] + sj[3:4]
        sq = d[0] * d[0] + d[1] * d[1] + d[2] * d[2]
        order = lax.broadcasted_iota(jnp.int32, (species_count, width), 0).astype(F32)
        t = (sq - order * spacing) / spacing
        basis = jnp.exp(-(t * t))
        b_hi = basis.astype(B16).astype(F32)
        b_lo = basis - b_hi
        b_zero = jnp.zeros_like(basis)
        latent = at_i[0:128] + at_j[0:128] + mul(
            radial_t, jnp.concatenate([b_hi, b_lo, b_hi, b_zero], axis=0).astype(B16)
        )
        s1 = gate(latent)
        first = latent * s1
        first2 = split(first)
        m = mul(mix_f[...], stack3(first2))
        s2 = gate(m)
        second = first + m * s2
        second2 = split(second)
        gains = mul(ch_f[...], stack3(second2))
        vg, tg = gains[0:128], gains[128:256]
        n = [x * (1.0 / CUTOFF) for x in d]
        ap = n[0] * pv[0] + n[1] * pv[1] + n[2] * pv[2]
        ac = n[0] * cv[0] + n[1] * cv[1] + n[2] * cv[2]
        ip = cv[0] * pv[0] + cv[1] * pv[1] + cv[2] * pv[2]
        ss = sq * (1.0 / (CUTOFF * CUTOFF))
        third = ss * (1.0 / 3.0)
        q = ac * ap - third * ip
        mixed = second + vg * ap + tg * q
        mixed2 = split(mixed)
        u = mul(read_f[...], stack3(mixed2))
        s3 = gate(u)
        h = u * s3
        readout = jnp.sum(out_col * h, axis=0, keepdims=True)
        env = 1.0 / (1.0 + ss)
        half_live = 0.5 * live
        halves = half_live * env * readout
        ge = half_live * pair_weight
        gr = ge * env
        acc_out[...] += h * gr
        du = (out_col * gr) * (s3 * (1.0 + u * (1.0 - s3)))
        du2 = split(du)
        gbuf[664:792] += outer3(mixed2, du2)
        dmixed = mul(read_b[...], stack3(du2))
        dq = dmixed * tg
        dap = dmixed * vg + dq * ac
        dac = dq * ap
        dip = -third * dq
        dss = -jnp.sum(dq * ip, axis=0, keepdims=True) * (1.0 / 3.0)
        dgain2 = split(jnp.concatenate([dmixed * ap, dmixed * q], axis=0))
        dch = outer3(second2, dgain2)
        gbuf[408:536] += dch[:, 0:128]
        gbuf[536:664] += dch[:, 128:256]
        dsecond = dmixed + mul(ch_b[...], stack3(dgain2))
        dm = dsecond * (s2 * (1.0 + m * (1.0 - s2)))
        dm2 = split(dm)
        gbuf[280:408] += outer3(first2, dm2)
        dfirst = dsecond + mul(mix_b[...], stack3(dm2))
        dlat = dfirst * (s1 * (1.0 + latent * (1.0 - s1)))
        lat2 = split(dlat)
        acc_rad[...] += outer3(lat2, split(jnp.concatenate([basis, b_zero], axis=0)))
        dbasis = mul(radial_b, stack3(lat2))[0:species_count]
        dsq = jnp.sum(dbasis * basis * t, axis=0, keepdims=True) * (-2.0 / spacing)
        dsq = dsq + (dss - ge * readout * env * env) * (1.0 / (CUTOFF * CUTOFF))
        dcv = [n[k] * dac + dip * pv[k] for k in range(3)]
        dpv = [n[k] * dap + dip * cv[k] for k in range(3)]
        dd = [
            jnp.sum(dac * cv[k] + dap * pv[k], axis=0, keepdims=True) * (1.0 / CUTOFF)
            + 2.0 * d[k] * dsq
            for k in range(3)
        ]

        def scatter(vector_parts, small_parts, one_hot):
            pieces = [lat2] + [split(v) for v in vector_parts]
            pieces.append(split(rows_of(small_parts, 16, width)))
            his = jnp.concatenate([p[0] for p in pieces], axis=0)
            los = jnp.concatenate([p[1] for p in pieces], axis=0)
            return mul_t(
                jnp.concatenate([his, los], axis=1), jnp.concatenate([one_hot, one_hot], axis=1)
            )

        acc_c[...] += scatter(dcv, [-dd[0], -dd[1], -dd[2], halves], oi)
        return scatter(dpv, dd + [halves], oj)

    slot = lax.broadcasted_iota(jnp.int32, (1, width), 1)

    def local_step(step, carry):
        start = pl.multiple_of(step * width, width)
        pairs = lp[:, pl.ds(start, width)]
        live = (slot + start < counts[0]).astype(F32)
        acc_p[...] += block(pairs[0:1], pairs[1:2], live, (0.0, 0.0, 0.0))
        return carry

    lax.fori_loop(0, lp.shape[1] // width, local_step, 0)

    sc2 = split(sc[...])
    gbuf[128:256] += outer3(sc2, split(acc_p[0:128]))
    gbuf[272:280] += mul_t(hot, acc_p[0:128], HIGHEST)

    returning = []
    for d in ORDER:
        for copy in inbound[d]:
            copy.wait()
        near_hot = hot_of(near[d, 512:520])
        near2 = split(near[d, 0:128])
        fill(there, mul(wp_t, stack3(near2)) + embed(emb[8:16], near_hot),
             near[d, 128:512], near[d, 512:520])
        live = (slot < counts[1 + d]).astype(F32)
        offsets = tuple(EDGE if k == d else 0.0 for k in range(3))
        ret[d] = block(fp[d, 0:1], fp[d, 1:2], live, offsets)
        copy = pltpu.make_async_remote_copy(
            src_ref=ret.at[d, 0:520],
            dst_ref=back.at[d],
            send_sem=ret_send.at[d],
            recv_sem=ret_recv.at[d],
            device_id=neighbour(d, 1),
            device_id_type=MESH,
        )
        copy.start()
        returning.append(copy)
        proj_grad = ret[d, 0:128]
        gbuf[128:256] += outer3(near2, split(proj_grad))
        gbuf[272:280] += mul_t(near_hot, proj_grad, HIGHEST)

    center_grad = acc_c[0:128]
    gbuf[0:128] += outer3(sc2, split(center_grad))
    gbuf[264:272] += mul_t(hot, center_grad, HIGHEST)
    lane = lax.broadcasted_iota(jnp.int32, (1, atom_slots), 1)
    valid = (lane < atoms[0]).astype(F32)
    weighted = small[3:4] * valid
    wide_hot = (
        lax.broadcasted_iota(jnp.int32, (atom_slots, atom_slots), 0).astype(F32) == small[4:5]
    ).astype(F32)
    out_grad = jnp.broadcast_to(jnp.sum(acc_out[...], axis=1, keepdims=True), (128, 128)).T[0:8]
    tail_row = lax.broadcasted_iota(jnp.int32, (8, 128), 0)
    gbuf[792:800] = jnp.where(tail_row == 0, out_grad, 0.0) + mul_t(
        rows_of([jnp.zeros_like(weighted), weighted], 8, atom_slots), wide_hot, HIGHEST
    )
    rad_wide = jnp.concatenate([acc_rad[...]] * 8, axis=1)
    gbuf[256:264] = rad_wide.T[0:species_count]

    def finish():
        for copy in returning:
            copy.wait()
        vgrad_out[...] = acc_c[128:512] + acc_p[128:512] + (
            back[0, 128:512] + back[1, 128:512] + back[2, 128:512]
        )
        tail = acc_c[512:520] + acc_p[512:520] + (
            back[0, 512:520] + back[1, 512:520] + back[2, 512:520]
        )
        pos_out[...] = tail[0:3]
        self_energy = jnp.zeros((1, atom_slots), F32)
        for s in range(species_count):
            self_energy = self_energy + jnp.where(small[4:5] == float(s), ref_e[s], 0.0)
        energy_out[...] = tail[3:4] + valid * self_energy
        partner = acc_p[0:128] + (back[0, 0:128] + back[1, 0:128] + back[2, 0:128])
        sgrad_out[...] = mul(weight3(wc[...]), stack3(split(acc_c[0:128]))) + mul(
            weight3(wp[...]), stack3(split(partner))
        )

    start, length, sem = 0, rows, 0
    held = []
    for p, phase in enumerate(phases):
        size = phase[2]
        chunk = length // size
        copies = []
        for k in range(1, size):
            q, t, target = peer(phase, k)
            copy = pltpu.make_async_remote_copy(
                src_ref=gbuf.at[pl.ds(pl.multiple_of(start + t * chunk, 8), chunk)],
                dst_ref=landing[p].at[k - 1],
                send_sem=rs_send.at[sem],
                recv_sem=rs_recv.at[sem],
                device_id=target,
                device_id_type=MESH,
            )
            copy.start()
            copies.append(copy)
            sem += 1
        q = peer(phase, 0)[0]
        start = start + q * chunk
        mine = pl.ds(pl.multiple_of(start, 8), chunk)
        if p == min(1, n_phases - 1):
            finish()
        for copy in copies:
            copy.wait()
        total = gbuf[mine, :]
        for k in range(size - 1):
            total = total + landing[p][k]
        if p == n_phases - 1:
            agb[mine, :] = total * (1.0 / (sizes[0] * sizes[1] * sizes[2]))
        else:
            gbuf[mine, :] = total
        held.append((phase, start, chunk))
        length = chunk
    sem = 0
    for phase, start, chunk in reversed(held):
        mine = pl.ds(pl.multiple_of(start, 8), chunk)
        copies = []
        for k in range(1, phase[2]):
            copy = pltpu.make_async_remote_copy(
                src_ref=agb.at[mine],
                dst_ref=agb.at[mine],
                send_sem=ag_send.at[sem],
                recv_sem=ag_recv.at[sem],
                device_id=peer(phase, k)[2],
                device_id_type=MESH,
            )
            copy.start()
            copies.append(copy)
            sem += 1
        for copy in copies:
            copy.wait()
    wgrad_out[...] = agb[0:800]


def per_device(scalars, vectors, positions, species, atom_count, energy_weight, local_pairs,
               face_pairs, tile_counts, w_center, w_partner, w_radial, species_embed, w_mix,
               w_channel, w_read, w_out, species_energy, *, sizes):
    channels, atom_slots = scalars.shape[3:]
    width = face_pairs.shape[-1]
    total = sizes[0] * sizes[1] * sizes[2]
    rows = -(-800 // (8 * total)) * 8 * total
    phases = phase_list(sizes)
    landing, length, n_sems = [], rows, 0
    for _, _, size in phases:
        length //= size
        landing.append(pltpu.VMEM((size - 1, length, 128), F32))
        n_sems += size - 1
    vmem = pl.BlockSpec(memory_space=pltpu.VMEM)
    smem = pl.BlockSpec(memory_space=pltpu.SMEM)
    hbm = pl.BlockSpec(memory_space=pltpu.HBM)
    dma = pltpu.SemaphoreType.DMA
    energy, pos, sgrad, vgrad, wgrad = pl.pallas_call(
        functools.partial(kernel, sizes, rows, width),
        out_shape=(
            jax.ShapeDtypeStruct((1, atom_slots), F32),
            jax.ShapeDtypeStruct((3, atom_slots), F32),
            jax.ShapeDtypeStruct((channels, atom_slots), F32),
            jax.ShapeDtypeStruct((3 * channels, atom_slots), F32),
            jax.ShapeDtypeStruct((800, 128), F32),
        ),
        in_specs=[hbm, hbm, hbm, hbm, hbm, hbm, hbm, smem, smem, hbm, hbm, vmem, vmem, hbm, hbm, hbm, vmem,
                  smem],
        out_specs=(vmem,) * 5,
        scratch_shapes=[
            pltpu.VMEM((528, 256), B16),
            pltpu.VMEM((528, 256), B16),
            pltpu.VMEM((3, 520, 128), F32),
            pltpu.VMEM((3, 528, 128), F32),
            pltpu.VMEM((3, 520, 128), F32),
            pltpu.VMEM((528, 128), F32),
            pltpu.VMEM((528, 128), F32),
            pltpu.VMEM((rows, 128), F32),
            pltpu.VMEM((rows, 128), F32),
            pltpu.VMEM((128, 384), B16),
            pltpu.VMEM((128, 384), B16),
            pltpu.VMEM((256, 384), B16),
            pltpu.VMEM((128, 768), B16),
            pltpu.VMEM((128, 384), B16),
            pltpu.VMEM((128, 384), B16),
            pltpu.VMEM((128, 128), F32),
            pltpu.VMEM((384, 128), F32),
            pltpu.VMEM(local_pairs.shape[3:], jnp.int32),
            pltpu.VMEM((3, 2, width), jnp.int32),
            pltpu.VMEM((128, 128), F32),
            pltpu.VMEM((128, 128), F32),
            pltpu.VMEM((128, 128), F32),
            pltpu.VMEM((256, 128), F32),
            pltpu.VMEM((128, 128), F32),
            pltpu.VMEM((128, width), F32),
            pltpu.VMEM((128, 16), F32),
            pltpu.VMEM((8, atom_slots), F32),
            pltpu.VMEM((3, atom_slots), F32),
            pltpu.VMEM((1, atom_slots), F32),
            pltpu.VMEM((1, atom_slots), jnp.int32),
        ] + landing + [
            dma((9,)), dma((9,)), dma((3,)), dma((3,)),
            dma((n_sems,)), dma((n_sems,)), dma((n_sems,)), dma((n_sems,)), dma((12,)),
        ],
        compiler_params=pltpu.CompilerParams(
            collective_id=0, has_side_effects=True, vmem_limit_bytes=63 * 1024 * 1024
        ),
    )(
        scalars[0, 0, 0],
        vectors[0, 0, 0].reshape(3 * channels, atom_slots),
        positions[0, 0, 0],
        energy_weight[0, 0],
        species[0, 0],
        local_pairs[0, 0, 0],
        face_pairs[0, 0, 0],
        tile_counts[0, 0, 0],
        atom_count[0, 0],
        w_center,
        w_partner,
        w_radial,
        species_embed.reshape(-1, channels),
        w_mix,
        w_channel.reshape(-1, channels),
        w_read,
        w_out[None, :],
        species_energy,
    )
    weight_count = sum(
        w.size for w in (w_center, w_partner, w_radial, species_embed, w_mix, w_channel, w_read,
                         w_out, species_energy)
    )
    return (
        energy[None, None],
        pos[None, None, None],
        sgrad[None, None, None],
        vgrad.reshape(3, channels, atom_slots)[None, None, None],
        wgrad.reshape(-1)[:weight_count],
    )


def solution(mesh):
    sizes = tuple(mesh.shape[a] for a in AXES)
    here = ("gx", "gy", "gz")
    return jax.shard_map(
        functools.partial(per_device, sizes=sizes),
        mesh=mesh,
        in_specs=(
            P(*here, None, None),
            P(*here, None, None, None),
            P(*here, None, None),
            P(*here, None),
            P(*here),
            P(*here, None),
            P(*here, None, None),
            P(*here, None, None, None),
            P(*here, None),
        ) + (P(),) * 9,
        out_specs=(
            P(*here, None),
            P(*here, None, None),
            P(*here, None, None),
            P(*here, None, None, None),
            P(),
        ),
        check_vma=False,
    )
```
